256 devices in a mesh: section: 4 (over y_hi, core), vocab: 32 (over x, z), hid: 2 (over y_lo).
Axes of the slice: x: 4, y: 4 (y_hi: 2, y_lo: 2; y = y_hi * 2 + y_lo), z: 8, core: 2. Of those that a mesh axis runs over, the one named last changes fastest.
Arguments:
- tokens: bfloat16 [1024, 7168], P(('section', 'vocab'), 'hid'), may hold values from -40 to 40, as said below
- gain: bfloat16 [7168], P('hid'), may hold values from 0.5 to 1.5
- head: bfloat16 [163840, 7168], P(('section', 'vocab'), 'hid'), may hold values from -1 to 1, as said below
Outputs:
- log_probs: float32 [1024, 163840], P('hid', ('section', 'vocab'))
The draws below stay inside these ranges and needn't reach their ends.
Inputs may be any that keep to these rules, and one draw needn't show every extreme that they name: `tokens`: hidden rows differ in scale from token to token. Rows of the head differ in scale.
All inputs are finite; a program needn't handle non-finite values.
Results may differ from the reference program's by a relative error of at most 0.00067.
Values may be sent and summed in bfloat16 or wider, within the bound.
No kernel may reach another device: no remote copies, remote signals or barrier semaphores. Data moves between devices by JAX's collectives and lax.ppermute only.
A program may use at most 64 MiB of HBM per device.

```python
import math
import jax
import jax.numpy as jnp
from jax import lax

D = 7168
V = 163840
TOKENS = 1024


def common_signs(key):
    return jax.random.rademacher(jax.random.fold_in(key, 29), (D,), jnp.float32)


def head_row(key, index):
    row_key = jax.random.fold_in(jax.random.fold_in(key, 11), index)
    noise_key, scale_key = jax.random.split(row_key)
    level = jnp.exp(math.log(3.0) * index.astype(jnp.float32) / V + jax.random.uniform(scale_key, (), jnp.float32) * math.log(3.0))
    values = jnp.clip(jax.random.normal(noise_key, (D,), jnp.float32), -6.0, 6.0)
    row = values * level / math.sqrt(D) + common_signs(key) * (256.0 / D)
    return jnp.clip(row, -1.0, 1.0)


def draw_head(key, part):
    rows = jax.vmap(lambda index: head_row(key, index))(jnp.arange(V, dtype=jnp.int32))
    return rows.astype(jnp.bfloat16)


def draw_tokens(key, part):
    shared = key
    signs = common_signs(shared)
    key = jax.random.fold_in(key, 3)
    base_key = jax.random.fold_in(key, 0)
    scale_key = jax.random.fold_in(key, 1)
    shift_key = jax.random.fold_in(key, 5)
    scales = jnp.exp(jax.random.uniform(scale_key, (TOKENS, 1), jnp.float32) * math.log(10.0))
    base = jnp.clip(jax.random.normal(base_key, (TOKENS, D), jnp.float32), -4.0, 4.0)
    values = base * scales
    shifted = jax.random.permutation(shift_key, TOKENS)[:8]
    mixing = (jnp.arange(8, dtype=jnp.float32) / 8.0)[:, None]
    lifted = (signs[None, :] + base[shifted] * mixing) * 4.0
    values = values.at[shifted].set(lifted)
    return jnp.clip(values, -40.0, 40.0).astype(jnp.bfloat16)


def setup_inputs(seed: int = 0) -> dict:
    seeds = jax.random.split(jax.random.key(seed), 4)
    tokens = draw_tokens(jax.random.fold_in(seeds[3], 71), 0)
    gain = jnp.clip(1.0 + 0.1 * jax.random.normal(seeds[1], (D,), jnp.float32), 0.5, 1.5).astype(jnp.bfloat16)
    head = draw_head(jax.random.fold_in(seeds[3], 71), 0)
    return {"tokens": tokens, "gain": gain, "head": head}


epsilon = 1e-06

def reference(tokens, gain, head):
    scaled = (tokens.astype(jnp.float32) * gain.astype(jnp.float32)).astype(jnp.bfloat16)
    squares = lax.optimization_barrier(jnp.sum(jnp.square(tokens.astype(jnp.float32)), axis=1))
    inv_rms = lax.rsqrt(squares / D + epsilon)
    raw = jnp.dot(scaled, head.T, preferred_element_type=jnp.float32)
    logits = raw * inv_rms[:, None]
    top = lax.optimization_barrier(jnp.max(logits, axis=1, keepdims=True))
    total = lax.optimization_barrier(jnp.sum(jnp.exp(logits - top), axis=1, keepdims=True))
    return logits - top - jnp.log(total)
```

```python
import itertools

import jax
import jax.numpy as jnp
from jax import lax
from jax.sharding import Mesh
from jax.sharding import PartitionSpec as P

D = 7168
epsilon = 1e-06
AXES = ("yh", "core", "x", "z", "h")
NY, NC, NX, NZ, NH = SIZES = (2, 2, 4, 8, 2)
SCALE = 0.125


def send(value, target):
    pairs = []
    for i, at in enumerate(itertools.product(*[range(n) for n in SIZES])):
        j = 0
        for a, n in zip(target(*at), SIZES):
            j = j * n + a % n
        pairs.append((i, j))
    return lax.ppermute(value, AXES, pairs)


def to_core(value):
    return send(value, lambda y, c, x, z, h: (y, c + 1, x, z, h))


def to_hid(value):
    return send(value, lambda y, c, x, z, h: (y, c, x, z, h + 1))


def along_z(value):
    return send(value, lambda y, c, x, z, h: (y, c, x, z + (1 if c == 0 else -1), h))


def split3(value):
    parts = []
    for _ in range(3):
        part = lax.reduce_precision(value, 8, 7)
        parts.append(part.astype(jnp.bfloat16))
        value = value - part
    return parts


def local(tokens, gain, head):
    yh, core, x, z, h = (lax.axis_index(a) for a in AXES)
    width = tokens.shape[1]
    f32 = tokens.astype(jnp.float32)
    scaled = (f32 * gain.astype(jnp.float32)).astype(jnp.bfloat16)
    squares = jnp.sum(jnp.square(f32), axis=1)
    pieces = jnp.stack(split3(squares), axis=1)
    own = jnp.concatenate([scaled, jnp.pad(pieces, ((0, 0), (0, 125)))], axis=1)
    other = send(own, lambda y, c, x, z, h: (y + 1, c, x, z, h))
    both = jnp.where(yh == h, jnp.concatenate([other, own]), jnp.concatenate([own, other]))
    column = lax.all_to_all(jnp.broadcast_to(both[None], (NX,) + both.shape), "x", 0, 0, tiled=True)
    swapped = to_core(column)
    cols = both.shape[1]

    def halves(first, second):
        return jnp.where(core == 0, first, second)

    plane = jnp.stack([halves(column, swapped), halves(swapped, column)])
    plane = plane.reshape(NC, NX, 2, 8, cols).transpose(2, 0, 1, 3, 4).reshape(128, cols)

    keep = jnp.zeros((NC, NX, NZ, 8, 1280), jnp.float32)
    keep_squares = jnp.zeros((NC, NX, NZ, 8), jnp.float32)
    got = jnp.zeros((NC, NX, NZ, 8, 1280), jnp.float16)
    aside = jnp.zeros((2, NC, NX, NZ, 8), jnp.float32)

    def squares_of(rows):
        return jnp.sum(rows[:, width : width + 3].astype(jnp.float32), axis=1)

    def product(rows):
        return lax.dot_general(rows[:, :width], head, (((1,), (1,)), ((), ())), preferred_element_type=jnp.float32)

    def put(into, value, at, lead=()):
        value = value.reshape(lead + (NC, NX, 1, 8) + value.shape[1 + len(lead) :])
        zero = jnp.int32(0)
        begin = [zero] * into.ndim
        begin[len(lead) + 2] = at
        return lax.dynamic_update_slice(into, value, begin)

    def work(chunk_s, chunk_k, places, state):
        keep, keep_squares, got, aside = state
        n = chunk_s.shape[0]
        partial = product(jnp.concatenate([chunk_s, chunk_k]))
        outward, stay = partial[:n], partial[n:]
        centre = jnp.mean(outward, axis=1)
        moved = to_hid(((outward - centre[:, None]) * SCALE).astype(jnp.float16))
        extra = jnp.stack([squares_of(chunk_s), centre])
        stay_squares = squares_of(chunk_k)
        for i, at in enumerate(places):
            part = slice(64 * i, 64 * i + 64)
            keep = put(keep, stay[part], at)
            keep_squares = put(keep_squares, stay_squares[part], at)
            got = put(got, moved[part], at)
            aside = put(aside, extra[:, part], at, (2,))
        return keep, keep_squares, got, aside

    state = (keep, keep_squares, got, aside)
    state = work(plane[:64], plane[64:], [z], state)
    block = plane
    for step in range(1, 4):
        block = along_z(block)
        second = to_core(block)
        away = jnp.where(core == 0, -step, step)
        places = [(z + away) % NZ, (z - away) % NZ]
        state = work(
            jnp.concatenate([block[:64], second[:64]]), jnp.concatenate([block[64:], second[64:]]), places, state
        )
    half = along_z(lax.dynamic_slice_in_dim(block, core * 64, 64))
    rest = to_core(half)
    keep, keep_squares, got, aside = work(halves(half, rest), halves(rest, half), [(z + 4) % NZ], state)

    aside = to_hid(aside)
    inv_rms = lax.rsqrt((keep_squares + aside[0]).reshape(512) / D + epsilon)
    raw = keep.reshape(512, 1280) + (got.reshape(512, 1280).astype(jnp.float32) / SCALE + aside[1].reshape(512, 1))
    logits = raw * inv_rms[:, None]
    top = jnp.max(logits, axis=1)
    total = jnp.sum(jnp.exp(logits - top[:, None]), axis=1)

    def merge(tops, totals):
        best = jnp.max(tops, axis=0)
        return best, jnp.sum(totals * jnp.exp(tops - best), axis=0)

    for axis in (0, 1):
        pair = jnp.stack([top, total])
        back = send(pair, lambda y, c, x, z, h: (y + 1 - axis, c + axis, x, z, h))
        top, total = merge(jnp.stack([top, back[0]]), jnp.stack([total, back[1]]))
    pair = jnp.stack([top, total])
    every = lax.all_to_all(jnp.broadcast_to(pair[None], (NX * NZ, 2, 512)), ("x", "z"), 0, 0, tiled=True)
    top, total = merge(every[:, 0], every[:, 1])
    return logits - top[:, None] - jnp.log(total)[:, None]


def solution(mesh):
    fine = Mesh(mesh.devices.reshape(SIZES), AXES)
    rows = ("yh", "core", "x", "z")
    return jax.shard_map(
        local,
        mesh=fine,
        in_specs=(P(rows, "h"), P("h"), P(rows, "h")),
        out_specs=P("h", rows),
        check_vma=False,
    )
```

```python
import functools
import itertools

import jax
import jax.numpy as jnp
from jax import lax
from jax.experimental import pallas as pl
from jax.experimental.pallas import tpu as pltpu
from jax.sharding import Mesh
from jax.sharding import PartitionSpec as P

D = 7168
epsilon = 1e-06
AXES = ("yh", "core", "x", "z", "h")
NY, NC, NX, NZ, NH = SIZES = (2, 2, 4, 8, 2)
HALF = 3584
VOCAB = 1280
ROWS = 512
LANES = 128
TILE = 256
WHOLE = pl.BlockSpec(memory_space=pltpu.VMEM)


def send(value, target):
    pairs = []
    for i, at in enumerate(itertools.product(*[range(n) for n in SIZES])):
        j = 0
        for a, n in zip(target(*at), SIZES):
            j = j * n + a % n
        pairs.append((i, j))
    return lax.ppermute(value, AXES, pairs)


def to_core(value):
    return send(value, lambda y, c, x, z, h: (y, c + 1, x, z, h))


def to_hid(value):
    return send(value, lambda y, c, x, z, h: (y, c, x, z, h + 1))


def along_z(value):
    return send(value, lambda y, c, x, z, h: (y, c, x, z + (1 if c == 0 else -1), h))


def along_x(value):
    return send(value, lambda y, c, x, z, h: (y, c, x + (1 if c == 0 else -1), z, h))


def split3(value):
    parts = []
    for _ in range(3):
        part = lax.reduce_precision(value, 8, 7)
        parts.append(part.astype(jnp.bfloat16))
        value = value - part
    return parts


def product_kernel(n_out, n_stay, *refs):
    outward, stay, (head_ref,) = refs[:n_out], refs[n_out : n_out + n_stay], refs[n_out + n_stay : n_out + n_stay + 1]
    sent_ref, rest = refs[n_out + n_stay + 1], refs[n_out + n_stay + 2 :]
    kept_ref, rows = (rest[0] if n_stay else None), rest[-1]
    at = 0
    for ref in outward + stay:
        n = ref.shape[0]
        rows[at : at + n] = ref[:, :HALF]
        at += n
    m = sent_ref.shape[0]
    centre = None
    for begin in range(0, VOCAB, TILE):
        columns = slice(begin, begin + TILE)
        part = lax.dot_general(
            rows[...], head_ref[columns, :], (((1,), (1,)), ((), ())), preferred_element_type=jnp.float32
        )
        if centre is None:
            centre = jnp.mean(part[:m], axis=1, keepdims=True)
        sent_ref[:, columns] = (part[:m] - centre).astype(jnp.bfloat16)
        if n_stay:
            kept_ref[:, columns] = part[m:]
    high = centre.astype(jnp.bfloat16).astype(jnp.float32)
    middle = (centre - high).astype(jnp.bfloat16).astype(jnp.float32)
    low = centre - high - middle
    at = 0
    for ref in outward:
        n = ref.shape[0]
        part = slice(at, at + n)
        lane = lax.broadcasted_iota(jnp.int32, (n, LANES), 1)
        extra = ref[:, HALF:].astype(jnp.float32)
        extra = jnp.where(lane == 0, high[part], jnp.where(lane == 1, middle[part], jnp.where(lane == 2, low[part], extra)))
        sent_ref[part, VOCAB:] = extra.astype(jnp.bfloat16)
        at += n
    at = 0
    for ref in stay:
        n = ref.shape[0]
        kept_ref[at : at + n, VOCAB:] = ref[:, HALF:].astype(jnp.float32)
        at += n


def product(outward, stay, head):
    m, k = (sum(a.shape[0] for a in arrays) for arrays in (outward, stay))
    shapes = [jax.ShapeDtypeStruct((m, VOCAB + LANES), jnp.bfloat16)]
    if stay:
        shapes.append(jax.ShapeDtypeStruct((k, VOCAB + LANES), jnp.float32))
    return pl.pallas_call(
        functools.partial(product_kernel, len(outward), len(stay)),
        in_specs=[WHOLE] * (len(outward) + len(stay) + 1),
        out_specs=[WHOLE] * len(shapes),
        out_shape=shapes,
        scratch_shapes=[pltpu.VMEM((m + k, HALF), jnp.bfloat16)],
        compiler_params=pltpu.CompilerParams(vmem_limit_bytes=30 * 2**20),
        cost_estimate=pl.CostEstimate(
            flops=2 * max(m + k, 256) * VOCAB * HALF, bytes_accessed=2 * VOCAB * HALF, transcendentals=0
        ),
        name="product",
    )(*outward, *stay, head)


def join_kernel(places, n_got, *refs):
    got, kept, (logits_ref, stats_ref, total) = refs[:n_got], refs[n_got:-3], refs[-3:]
    core, x, z = (lax.axis_index(a) for a in ("core", "x", "z"))
    mine = jnp.where(core == 0, -1, 1)
    for first, refs in ((True, got), (False, kept)):
        for ref, groups in zip(refs, places[0 if first else 1]):
            for begin, blocks in groups:
                count = len(blocks)
                value = ref[begin : begin + 8 * count, :].astype(jnp.float32)
                for i, (c, (dx, sx), (dz, sz)) in enumerate(blocks):
                    x_at = lax.rem(x + dx + sx * mine + 2 * NX, NX)
                    z_at = lax.rem(z + dz + sz * mine + 2 * NZ, NZ)
                    at = pl.ds(pl.multiple_of(((c * NX + x_at) * NZ + z_at) * 8, 8), 8)
                    block = value[8 * i : 8 * i + 8]
                    if first:
                        total[at, :] = block
                    else:
                        total[at, :] = total[at, :] + block
    step = 128
    for begin in range(0, ROWS, step):
        rows = slice(begin, begin + step)
        extra = total[rows, VOCAB:]
        lane = lax.broadcasted_iota(jnp.int32, (step, LANES), 1)
        centre = jnp.sum(jnp.where(lane < 3, extra, 0.0), axis=1, keepdims=True)
        squares = jnp.sum(jnp.where(lane < 3, 0.0, extra), axis=1, keepdims=True)
        inv_rms = lax.rsqrt(squares / D + epsilon)
        logits = (total[rows, :VOCAB] + centre) * inv_rms
        top = jnp.max(logits, axis=1, keepdims=True)
        summed = jnp.sum(jnp.exp(logits - top), axis=1, keepdims=True)
        logits_ref[rows, :] = logits
        pair = jnp.where(lane == 0, top, summed)
        stats_ref[:, rows] = pair.T[:8]


def join(places, got, kept):
    return pl.pallas_call(
        functools.partial(join_kernel, places, len(got)),
        in_specs=[WHOLE] * (len(got) + len(kept)),
        out_specs=[WHOLE] * 2,
        out_shape=[
            jax.ShapeDtypeStruct((ROWS, VOCAB), jnp.float32),
            jax.ShapeDtypeStruct((8, ROWS), jnp.float32),
        ],
        scratch_shapes=[pltpu.VMEM((ROWS, VOCAB + LANES), jnp.float32)],
        compiler_params=pltpu.CompilerParams(vmem_limit_bytes=30 * 2**20),
        name="join",
    )(*got, *kept)


def local(tokens, gain, head):
    yh, core, h = (lax.axis_index(a) for a in ("yh", "core", "h"))
    f32 = tokens.astype(jnp.float32)
    scaled = (f32 * gain.astype(jnp.float32)).astype(jnp.bfloat16)
    squares = jnp.sum(jnp.square(f32), axis=1)
    pieces = jnp.stack(split3(squares), axis=1)
    own = jnp.concatenate([scaled, jnp.pad(pieces, ((0, 0), (3, LANES - 6)))], axis=1)

    first = core == 0

    def cat(*arrays):
        return jnp.concatenate(arrays)

    def by_core(mine, other):
        return jnp.where(first, mine, other), jnp.where(first, other, mine)

    from_y = send(own, lambda y, c, x, z, h: (y + 1, c, x, z, h))
    from_c = to_core(own)
    from_yc = send(own, lambda y, c, x, z, h: (y + 1, c + 1, x, z, h))
    stays = yh == h
    out_mine, out_other = jnp.where(stays, from_y, own), jnp.where(stays, from_yc, from_c)
    stay_mine, stay_other = jnp.where(stays, own, from_y), jnp.where(stays, from_c, from_yc)
    out16 = cat(*by_core(out_mine, out_other))
    stay16 = cat(*by_core(stay_mine, stay_other))

    near = along_x(out16)
    far = send(out_mine, lambda y, c, x, z, h: (y, c, x + 2, z, h))
    ring = [along_z(stay16)]
    side = cat(near, far)
    other_side = to_core(side)
    out64 = cat(out16, *by_core(side[:16], other_side[:16]), *by_core(side[16:], other_side[16:]))
    ring.append(along_z(ring[-1]))
    block = along_z(out64)
    ring.append(along_z(ring[-1]))
    ring.append(along_z(jnp.where(first, ring[-1][:8], ring[-1][8:])))
    ring = cat(*ring)
    other_ring = to_core(ring)
    stay128 = [stay16]
    for step in range(3):
        part = slice(16 * step, 16 * step + 16)
        stay128 += by_core(ring[part], other_ring[part])
    stay128 = cat(*stay128, *by_core(ring[48:], other_ring[48:]))

    side_x = along_x(stay128)
    sides = [(block, to_core(block))]
    block = along_z(block)
    got, kept = [], []

    def work(outward, stay):
        sent, *rest = product(outward, stay, head)
        got.append(to_hid(sent))
        kept.extend(rest)

    work([out64, *sides[0]], [stay128])
    sides.append((block, to_core(block)))
    block = along_z(block)
    work(list(sides[1]), [])
    sides_x = (side_x, to_core(side_x))
    far_x = along_x(jnp.where(first, side_x[:64], side_x[64:]))
    sides.append((block, to_core(block)))
    far_z = along_z(jnp.where(first, block[:32], block[32:]))
    work(list(sides[2]), list(sides_x))
    last_z = cat(*by_core(far_z, to_core(far_z)))
    last_x = cat(*by_core(far_x, to_core(far_x)))
    work([last_z], [last_x])

    def plane(dz, sz):
        return [(c, (dx, 0), (dz, sz)) for dx in (0, -1, 1, 2) for c in range(NC)]

    def column(dx, sx):
        return [(c, (dx, sx), (dz, 0)) for dz in (0, -1, 1, -2, 2, -3, 3, 4) for c in range(NC)]

    places = (
        (
            ((0, plane(0, 0)), (64, plane(0, 1)), (128, plane(0, -1))),
            ((0, plane(0, 2)), (64, plane(0, -2))),
            ((0, plane(0, 3)), (64, plane(0, -3))),
            ((0, plane(4, 0)),),
        ),
        (
            ((0, column(0, 0)),),
            ((0, column(0, 1)), (128, column(0, -1))),
            ((0, column(2, 0)),),
        ),
    )
    logits, stats = join(places, got, kept)

    def merge(pairs):
        best = jnp.max(pairs[:, 0], axis=0)
        return jnp.stack([best, jnp.sum(pairs[:, 1] * jnp.exp(pairs[:, 0] - best), axis=0)])

    pair = stats[:2]
    section = [pair] + [
        send(pair, lambda y, c, x, z, h: (y + dy, c + dc, x, z, h)) for dy, dc in ((0, 1), (1, 0), (1, 1))
    ]
    pair = merge(jnp.stack(section))
    every = lax.all_to_all(jnp.broadcast_to(pair[None], (NX * NZ, 2, ROWS)), ("x", "z"), 0, 0, tiled=True)
    top, total = merge(every)
    return logits - top[:, None] - jnp.log(total)[:, None]


def solution(mesh):
    fine = Mesh(mesh.devices.reshape(SIZES), AXES)
    rows = ("yh", "core", "x", "z")
    return jax.shard_map(
        local,
        mesh=fine,
        in_specs=(P(rows, "h"), P("h"), P(rows, "h")),
        out_specs=P("h", rows),
        check_vma=False,
    )
```

```python
import functools
import itertools

import jax
import jax.numpy as jnp
from jax import lax
from jax.experimental import pallas as pl
from jax.experimental.pallas import tpu as pltpu
from jax.sharding import Mesh
from jax.sharding import PartitionSpec as P

D = 7168
epsilon = 1e-06
AXES = ("yh", "core", "x", "z", "h")
NY, NC, NX, NZ, NH = SIZES = (2, 2, 4, 8, 2)
HALF = 3584
VOCAB = 1280
ROWS = 512
LANES = 128
REACH = 80.0
TILE = 256
WHOLE = pl.BlockSpec(memory_space=pltpu.VMEM)


def send(value, target):
    pairs = []
    for i, at in enumerate(itertools.product(*[range(n) for n in SIZES])):
        j = 0
        for a, n in zip(target(*at), SIZES):
            j = j * n + a % n
        pairs.append((i, j))
    return lax.ppermute(value, AXES, pairs)


def to_core(value):
    return send(value, lambda y, c, x, z, h: (y, c + 1, x, z, h))


def to_hid(value):
    return send(value, lambda y, c, x, z, h: (y, c, x, z, h + 1))


def along_z(value, hops=1):
    return send(value, lambda y, c, x, z, h: (y, c, x, z + (hops if c == 0 else -hops), h))


def along_x(value):
    return send(value, lambda y, c, x, z, h: (y, c, x + (1 if c == 0 else -1), z, h))


def split3(value):
    parts = []
    for _ in range(3):
        part = lax.reduce_precision(value, 8, 7)
        parts.append(part.astype(jnp.bfloat16))
        value = value - part
    return parts


def split3_in_kernel(value):
    high = value.astype(jnp.bfloat16).astype(jnp.float32)
    middle = (value - high).astype(jnp.bfloat16).astype(jnp.float32)
    return high, middle, value - high - middle


def product_kernel(n_blocks, *refs):
    outward, stay, (head_ref, sent_ref, kept_ref, rows, raw) = refs[:n_blocks], refs[n_blocks:-5], refs[-5:]
    m = sent_ref.shape[0]
    at = 0
    for ref in outward + stay:
        n = ref.shape[0]
        rows[at : at + n] = ref[:, :HALF]
        if at >= m:
            kept_ref[at - m : at - m + n, VOCAB:] = ref[:, HALF:].astype(jnp.float32)
        at += n
    for begin in range(0, VOCAB, TILE):
        columns = slice(begin, begin + TILE)
        part = lax.dot_general(
            rows[...], head_ref[columns, :], (((1,), (1,)), ((), ())), preferred_element_type=jnp.float32
        )
        raw[:, columns] = part[:m]
        kept_ref[:, columns] = part[m:]
    at = 0
    for ref in outward:
        for begin in range(0, ref.shape[0], 32):
            part = slice(at, at + 32)
            value = raw[part, :]
            high = jnp.max(value, axis=1, keepdims=True)
            low = jnp.min(value, axis=1, keepdims=True)
            centre = 0.5 * (high + low)
            unit = jnp.maximum((high - low) * (0.5 / REACH), 1e-30)
            sent_ref[part, :VOCAB] = jnp.exp((value - centre) * (1.0 / unit)).astype(jnp.bfloat16)
            lane = lax.broadcasted_iota(jnp.int32, (32, LANES), 1)
            extra = ref[begin : begin + 32, HALF:].astype(jnp.float32)
            for where, number in ((0, centre), (6, unit)):
                for i, piece in enumerate(split3_in_kernel(number)):
                    extra = jnp.where(lane == where + i, piece, extra)
            sent_ref[part, VOCAB:] = extra.astype(jnp.bfloat16)
            at += 32


def product(outward, stay, head):
    m = sum(a.shape[0] for a in outward)
    return pl.pallas_call(
        functools.partial(product_kernel, len(outward)),
        in_specs=[WHOLE] * (2 * len(outward) + 1),
        out_specs=[WHOLE] * 2,
        out_shape=[
            jax.ShapeDtypeStruct((m, VOCAB + LANES), jnp.bfloat16),
            jax.ShapeDtypeStruct((m, VOCAB + LANES), jnp.float32),
        ],
        scratch_shapes=[pltpu.VMEM((2 * m, HALF), jnp.bfloat16), pltpu.VMEM((m, VOCAB), jnp.float32)],
        compiler_params=pltpu.CompilerParams(vmem_limit_bytes=30 * 2**20),
        cost_estimate=pl.CostEstimate(flops=1, bytes_accessed=1, transcendentals=0),
        name="product",
    )(*outward, *stay, head)


def join_kernel(places, n_got, *refs):
    got, kept, (logits_ref, stats_ref, total) = refs[:n_got], refs[n_got:-3], refs[-3:]
    core, x, z = (lax.axis_index(a) for a in ("core", "x", "z"))
    mine = jnp.where(core == 0, -1, 1)
    for first, refs in ((True, got), (False, kept)):
        for ref, groups in zip(refs, places):
            for begin, blocks in zip(range(0, ref.shape[0], 64), groups):
                value = ref[begin : begin + 64, :VOCAB].astype(jnp.float32)
                extra = ref[begin : begin + 64, VOCAB:].astype(jnp.float32)
                if first:
                    lane = lax.broadcasted_iota(jnp.int32, extra.shape, 1)
                    centre = jnp.sum(jnp.where(lane < 3, extra, 0.0), axis=1, keepdims=True)
                    unit = jnp.sum(jnp.where(lane < 6, 0.0, extra), axis=1, keepdims=True)
                    extra = jnp.where((lane >= 3) & (lane < 6), extra, 0.0)
                    value = jnp.log(value) * unit + centre
                for i, (c, dx, (dz, sz)) in enumerate(blocks):
                    x_at = lax.rem(x + dx + NX, NX)
                    z_at = lax.rem(z + dz + sz * mine + NZ, NZ)
                    at = pl.ds(pl.multiple_of(((c * NX + x_at) * NZ + z_at) * 8, 8), 8)
                    eight = slice(8 * i, 8 * i + 8)
                    if first:
                        total[at, :VOCAB] = value[eight]
                        total[at, VOCAB:] = extra[eight]
                    else:
                        total[at, :VOCAB] += value[eight]
                        total[at, VOCAB:] += extra[eight]
    step = 128
    for begin in range(0, ROWS, step):
        rows = slice(begin, begin + step)
        lane = lax.broadcasted_iota(jnp.int32, (step, LANES), 1)
        squares = jnp.sum(total[rows, VOCAB:], axis=1, keepdims=True)
        inv_rms = lax.rsqrt(squares / D + epsilon)
        logits = total[rows, :VOCAB] * inv_rms
        top = jnp.max(logits, axis=1, keepdims=True)
        summed = jnp.sum(jnp.exp(logits - top), axis=1, keepdims=True)
        logits_ref[rows, :] = logits
        pair = jnp.where(lane == 0, top, summed)
        stats_ref[:, rows] = pair.T[:8]


def join(places, got, kept):
    return pl.pallas_call(
        functools.partial(join_kernel, places, len(got)),
        in_specs=[WHOLE] * (len(got) + len(kept)),
        out_specs=[WHOLE] * 2,
        out_shape=[
            jax.ShapeDtypeStruct((ROWS, VOCAB), jnp.float32),
            jax.ShapeDtypeStruct((8, ROWS), jnp.float32),
        ],
        scratch_shapes=[pltpu.VMEM((ROWS, VOCAB + LANES), jnp.float32)],
        compiler_params=pltpu.CompilerParams(vmem_limit_bytes=30 * 2**20),
        name="join",
    )(*got, *kept)


def touch_kernel(rows_ref, head_ref, out_ref):
    out_ref[...] = rows_ref[...]


def touch(rows, head):
    return pl.pallas_call(
        touch_kernel,
        in_specs=[WHOLE] * 2,
        out_specs=WHOLE,
        out_shape=jax.ShapeDtypeStruct(rows.shape, rows.dtype),
        compiler_params=pltpu.CompilerParams(vmem_limit_bytes=16 * 2**20),
        name="touch",
    )(rows, head)


def local(tokens, gain, head):
    yh, core, h = (lax.axis_index(a) for a in ("yh", "core", "h"))
    f32 = tokens.astype(jnp.float32)
    scaled = (f32 * gain.astype(jnp.float32)).astype(jnp.bfloat16)
    squares = jnp.sum(jnp.square(f32), axis=1)
    pieces = jnp.stack(split3(squares), axis=1)
    own = jnp.concatenate([scaled, jnp.pad(pieces, ((0, 0), (3, LANES - 6)))], axis=1)

    first = core == 0

    def cat(*arrays):
        return jnp.concatenate(arrays)

    def by_core(mine, other):
        return jnp.where(first, mine, other), jnp.where(first, other, mine)

    from_y = send(own, lambda y, c, x, z, h: (y + 1, c, x, z, h))
    from_c = to_core(own)
    from_yc = send(own, lambda y, c, x, z, h: (y + 1, c + 1, x, z, h))
    flag = touch(jnp.full((8, LANES), yh == h, jnp.float32), head)
    stays = flag[:1, :1] > 0.5
    out_mine, out_other = jnp.where(stays, from_y, own), jnp.where(stays, from_yc, from_c)
    stay_mine, stay_other = jnp.where(stays, own, from_y), jnp.where(stays, from_c, from_yc)
    out16 = cat(*by_core(out_mine, out_other))
    stay16 = cat(*by_core(stay_mine, stay_other))

    after = lax.optimization_barrier

    near = along_x(cat(out16, stay16))
    far = send(cat(out_mine, stay_mine), lambda y, c, x, z, h: (y, c, x + 2, z, h))
    side = cat(near, far)
    other_side = to_core(side)
    planes = []
    for own16, near_at, far_at in ((out16, 0, 32), (stay16, 16, 40)):
        parts = [own16]
        for part in (slice(near_at, near_at + 16), slice(far_at, far_at + 8)):
            parts += by_core(side[part], other_side[part])
        planes.append(cat(*parts))

    got, kept = [], []

    def work(outward, stay):
        sent, rest = product(outward, stay, head)
        got.append(to_hid(sent))
        kept.append(rest)
        return sent

    out, stay = (along_z(a) for a in planes)
    sent = work(planes[:1], planes[1:])
    for step in range(1, 4):
        out_later = along_z(out if step < 3 else jnp.where(first, out[:32], out[32:]))
        out_other = to_core(out)
        stay, sent = after((stay, sent))
        if step > 1:
            stay, got[step - 2] = after((stay, got[step - 2]))
        stay_later = along_z(stay if step < 3 else jnp.where(first, stay[:32], stay[32:]))
        sent = work([out, out_other], [stay, to_core(stay)])
        out, stay = out_later, stay_later
    out_other = to_core(out)
    stay, sent, got[2] = after((stay, sent, got[2]))
    work([cat(*by_core(out, out_other))], [cat(*by_core(stay, to_core(stay)))])

    def rows_of(*shifts):
        return [[(c, dx, shift) for dx in (0, -1, 1, 2) for c in range(NC)] for shift in shifts]

    places = [rows_of((0, 0))] + [rows_of((0, step), (0, -step)) for step in range(1, 4)] + [rows_of((4, 0))]
    logits, stats = join(places, got, kept)

    def merge(pairs):
        best = jnp.max(pairs[:, 0], axis=0)
        return jnp.stack([best, jnp.sum(pairs[:, 1] * jnp.exp(pairs[:, 0] - best), axis=0)])

    pair = stats[:2]
    section = [pair] + [
        send(pair, lambda y, c, x, z, h: (y + dy, c + dc, x, z, h)) for dy, dc in ((0, 1), (1, 0), (1, 1))
    ]
    pair = merge(jnp.stack(section))
    every = lax.all_to_all(jnp.broadcast_to(pair[None], (NX * NZ, 2, ROWS)), ("x", "z"), 0, 0, tiled=True)
    top, total = merge(every)
    return logits - top[:, None] - jnp.log(total)[:, None]


def solution(mesh):
    fine = Mesh(mesh.devices.reshape(SIZES), AXES)
    rows = ("yh", "core", "x", "z")
    return jax.shard_map(
        local,
        mesh=fine,
        in_specs=(P(rows, "h"), P("h"), P(rows, "h")),
        out_specs=P("h", rows),
        check_vma=False,
    )
```

```python
import functools
import itertools

import jax
import jax.numpy as jnp
from jax import lax
from jax.experimental import pallas as pl
from jax.experimental.pallas import tpu as pltpu
from jax.sharding import Mesh
from jax.sharding import PartitionSpec as P

D = 7168
epsilon = 1e-06
AXES = ("yh", "core", "x", "z", "h")
NY, NC, NX, NZ, NH = SIZES = (2, 2, 4, 8, 2)
HALF = 3584
VOCAB = 1280
ROWS = 512
LANES = 128
REACH = 80.0
TILE = 256
WHOLE = pl.BlockSpec(memory_space=pltpu.VMEM)


def send(value, target):
    pairs = []
    for i, at in enumerate(itertools.product(*[range(n) for n in SIZES])):
        j = 0
        for a, n in zip(target(*at), SIZES):
            j = j * n + a % n
        pairs.append((i, j))
    return lax.ppermute(value, AXES, pairs)


def to_core(value):
    return send(value, lambda y, c, x, z, h: (y, c + 1, x, z, h))


def to_hid(value):
    return send(value, lambda y, c, x, z, h: (y, c, x, z, h + 1))


def along_z(value, hops=1):
    return send(value, lambda y, c, x, z, h: (y, c, x, z + (hops if c == 0 else -hops), h))


def along_x(value):
    return send(value, lambda y, c, x, z, h: (y, c, x + (1 if c == 0 else -1), z, h))


def split3(value):
    parts = []
    for _ in range(3):
        part = lax.reduce_precision(value, 8, 7)
        parts.append(part.astype(jnp.bfloat16))
        value = value - part
    return parts


def split3_in_kernel(value):
    high = value.astype(jnp.bfloat16).astype(jnp.float32)
    middle = (value - high).astype(jnp.bfloat16).astype(jnp.float32)
    return high, middle, value - high - middle


def product_kernel(n_blocks, *refs):
    outward, stay, (head_ref, sent_ref, kept_ref, rows, raw) = refs[:n_blocks], refs[n_blocks:-5], refs[-5:]
    m = sent_ref.shape[0]
    at = 0
    for ref in outward + stay:
        n = ref.shape[0]
        rows[at : at + n] = ref[:, :HALF]
        if at >= m:
            kept_ref[at - m : at - m + n, VOCAB:] = ref[:, HALF:].astype(jnp.float32)
        at += n
    for begin in range(0, VOCAB, TILE):
        columns = slice(begin, begin + TILE)
        part = lax.dot_general(
            rows[...], head_ref[columns, :], (((1,), (1,)), ((), ())), preferred_element_type=jnp.float32
        )
        raw[:, columns] = part[:m]
        kept_ref[:, columns] = part[m:]
    at = 0
    for ref in outward:
        for begin in range(0, ref.shape[0], 32):
            part = slice(at, at + 32)
            value = raw[part, :]
            high = jnp.max(value, axis=1, keepdims=True)
            low = jnp.min(value, axis=1, keepdims=True)
            centre = 0.5 * (high + low)
            unit = jnp.maximum((high - low) * (0.5 / REACH), 1e-30)
            sent_ref[part, :VOCAB] = jnp.exp((value - centre) * (1.0 / unit)).astype(jnp.bfloat16)
            lane = lax.broadcasted_iota(jnp.int32, (32, LANES), 1)
            extra = ref[begin : begin + 32, HALF:].astype(jnp.float32)
            for where, number in ((0, centre), (6, unit)):
                for i, piece in enumerate(split3_in_kernel(number)):
                    extra = jnp.where(lane == where + i, piece, extra)
            sent_ref[part, VOCAB:] = extra.astype(jnp.bfloat16)
            at += 32


def product(outward, stay, head):
    m = sum(a.shape[0] for a in outward)
    return pl.pallas_call(
        functools.partial(product_kernel, len(outward)),
        in_specs=[WHOLE] * (2 * len(outward) + 1),
        out_specs=[WHOLE] * 2,
        out_shape=[
            jax.ShapeDtypeStruct((m, VOCAB + LANES), jnp.bfloat16),
            jax.ShapeDtypeStruct((m, VOCAB + LANES), jnp.float32),
        ],
        scratch_shapes=[pltpu.VMEM((2 * m, HALF), jnp.bfloat16), pltpu.VMEM((m, VOCAB), jnp.float32)],
        compiler_params=pltpu.CompilerParams(vmem_limit_bytes=30 * 2**20),
        cost_estimate=pl.CostEstimate(flops=1, bytes_accessed=1, transcendentals=0),
        name="product",
    )(*outward, *stay, head)


def join_kernel(places, n_got, *refs):
    got, kept, (logits_ref, stats_ref, total) = refs[:n_got], refs[n_got:-3], refs[-3:]
    core, x, z = (lax.axis_index(a) for a in ("core", "x", "z"))
    mine = jnp.where(core == 0, -1, 1)
    for first, refs in ((True, got), (False, kept)):
        for ref, groups in zip(refs, places):
            for begin, blocks in zip(range(0, ref.shape[0], 64), groups):
                value = ref[begin : begin + 64, :VOCAB].astype(jnp.float32)
                extra = ref[begin : begin + 64, VOCAB:].astype(jnp.float32)
                if first:
                    lane = lax.broadcasted_iota(jnp.int32, extra.shape, 1)
                    centre = jnp.sum(jnp.where(lane < 3, extra, 0.0), axis=1, keepdims=True)
                    unit = jnp.sum(jnp.where(lane < 6, 0.0, extra), axis=1, keepdims=True)
                    extra = jnp.where((lane >= 3) & (lane < 6), extra, 0.0)
                    value = jnp.log(value) * unit + centre
                for i, (c, dx, (dz, sz)) in enumerate(blocks):
                    x_at = lax.rem(x + dx + NX, NX)
                    z_at = lax.rem(z + dz + sz * mine + NZ, NZ)
                    at = pl.ds(pl.multiple_of(((c * NX + x_at) * NZ + z_at) * 8, 8), 8)
                    eight = slice(8 * i, 8 * i + 8)
                    if first:
                        total[at, :VOCAB] = value[eight]
                        total[at, VOCAB:] = extra[eight]
                    else:
                        total[at, :VOCAB] += value[eight]
                        total[at, VOCAB:] += extra[eight]
    step = 128
    for begin in range(0, ROWS, step):
        rows = slice(begin, begin + step)
        lane = lax.broadcasted_iota(jnp.int32, (step, LANES), 1)
        squares = jnp.sum(total[rows, VOCAB:], axis=1, keepdims=True)
        inv_rms = lax.rsqrt(squares / D + epsilon)
        logits = total[rows, :VOCAB] * inv_rms
        top = jnp.max(logits, axis=1, keepdims=True)
        summed = jnp.sum(jnp.exp(logits - top), axis=1, keepdims=True)
        logits_ref[rows, :] = logits
        pair = jnp.where(lane == 0, top, summed)
        pair = pair.T
        at = begin // step
        stats_ref[at : at + 1, :] = pair[:1]
        stats_ref[4 + at : 5 + at, :] = pair[1:2]


def join(places, got, kept):
    return pl.pallas_call(
        functools.partial(join_kernel, places, len(got)),
        in_specs=[WHOLE] * (len(got) + len(kept)),
        out_specs=[WHOLE] * 2,
        out_shape=[
            jax.ShapeDtypeStruct((ROWS, VOCAB), jnp.float32),
            jax.ShapeDtypeStruct((8, LANES), jnp.float32),
        ],
        scratch_shapes=[pltpu.VMEM((ROWS, VOCAB + LANES), jnp.float32)],
        compiler_params=pltpu.CompilerParams(vmem_limit_bytes=30 * 2**20),
        name="join",
    )(*got, *kept)


def local(tokens, gain, head):
    yh, core, h = (lax.axis_index(a) for a in ("yh", "core", "h"))
    f32 = tokens.astype(jnp.float32)
    scaled = (f32 * gain.astype(jnp.float32)).astype(jnp.bfloat16)
    squares = jnp.sum(jnp.square(f32), axis=1)
    pieces = jnp.stack(split3(squares), axis=1)
    own = jnp.concatenate([scaled, jnp.pad(pieces, ((0, 0), (3, LANES - 6)))], axis=1)

    first = core == 0

    def cat(*arrays):
        return jnp.concatenate(arrays)

    def by_core(mine, other):
        return jnp.where(first, mine, other), jnp.where(first, other, mine)

    from_y = send(own, lambda y, c, x, z, h: (y + 1, c, x, z, h))
    from_c = to_core(own)
    from_yc = send(own, lambda y, c, x, z, h: (y + 1, c + 1, x, z, h))
    stays = yh == h
    out_mine, out_other = jnp.where(stays, from_y, own), jnp.where(stays, from_yc, from_c)
    stay_mine, stay_other = jnp.where(stays, own, from_y), jnp.where(stays, from_c, from_yc)
    out16 = cat(*by_core(out_mine, out_other))
    stay16 = cat(*by_core(stay_mine, stay_other))

    after = lax.optimization_barrier

    planes = []
    for own16, own8 in ((out16, out_mine), (stay16, stay_mine)):
        side = cat(along_x(own16), send(own8, lambda y, c, x, z, h: (y, c, x + 2, z, h)))
        other_side = to_core(side)
        parts = by_core(side[:16], other_side[:16]) + by_core(side[16:], other_side[16:])
        planes.append(cat(own16, *parts))

    got, kept = [], []

    def work(outward, stay):
        sent, rest = product(outward, stay, head)
        got.append(to_hid(sent))
        kept.append(rest)
        return sent

    out, stay = (along_z(a) for a in planes)
    sent = work(planes[:1], planes[1:])
    out, sent = after((out, sent))
    for step in range(1, 4):
        out_later = along_z(out if step < 3 else jnp.where(first, out[:32], out[32:]))
        out_other = to_core(out)
        stay, sent = after((stay, sent))
        if step > 1:
            stay, got[step - 2] = after((stay, got[step - 2]))
        stay_later = along_z(stay if step < 3 else jnp.where(first, stay[:32], stay[32:]))
        sent = work([out, out_other], [stay, to_core(stay)])
        out, stay = out_later, stay_later
    out_other = to_core(out)
    stay, sent, got[2] = after((stay, sent, got[2]))
    work([cat(*by_core(out, out_other))], [cat(*by_core(stay, to_core(stay)))])

    def rows_of(*shifts):
        return [[(c, dx, shift) for dx in (0, -1, 1, 2) for c in range(NC)] for shift in shifts]

    places = [rows_of((0, 0))] + [rows_of((0, step), (0, -step)) for step in range(1, 4)] + [rows_of((4, 0))]
    logits, stats = join(places, got, kept)

    def merge(pairs):
        best = jnp.max(pairs[:, :4], axis=0)
        return jnp.concatenate([best, jnp.sum(pairs[:, 4:] * jnp.exp(pairs[:, :4] - best), axis=0)])

    section = [stats] + [
        send(stats, lambda y, c, x, z, h: (y + dy, c + dc, x, z, h)) for dy, dc in ((0, 1), (1, 0), (1, 1))
    ]
    stats = merge(jnp.stack(section))
    every = lax.all_to_all(jnp.broadcast_to(stats[None], (NX * NZ, 8, LANES)), ("x", "z"), 0, 0, tiled=True)
    stats = merge(every)
    top, total = stats[:4].reshape(ROWS, 1), stats[4:].reshape(ROWS, 1)
    return logits - top - jnp.log(total)


def solution(mesh):
    fine = Mesh(mesh.devices.reshape(SIZES), AXES)
    rows = ("yh", "core", "x", "z")
    return jax.shard_map(
        local,
        mesh=fine,
        in_specs=(P(rows, "h"), P("h"), P(rows, "h")),
        out_specs=P("h", rows),
        check_vma=False,
    )
```

```python
import functools
import itertools

import jax
import jax.numpy as jnp
from jax import lax
from jax.experimental import pallas as pl
from jax.experimental.pallas import tpu as pltpu
from jax.sharding import Mesh
from jax.sharding import PartitionSpec as P

D = 7168
epsilon = 1e-06
AXES = ("yh", "core", "x", "z", "h")
NY, NC, NX, NZ, NH = SIZES = (2, 2, 4, 8, 2)
HALF = 3584
VOCAB = 1280
ROWS = 512
LANES = 128
REACH = 80.0
TILE = 256
WHOLE = pl.BlockSpec(memory_space=pltpu.VMEM)


def send(value, target):
    pairs = []
    for i, at in enumerate(itertools.product(*[range(n) for n in SIZES])):
        j = 0
        for a, n in zip(target(*at), SIZES):
            j = j * n + a % n
        pairs.append((i, j))
    return lax.ppermute(value, AXES, pairs)


def to_core(value):
    return send(value, lambda y, c, x, z, h: (y, c + 1, x, z, h))


def to_hid(value):
    return send(value, lambda y, c, x, z, h: (y, c, x, z, h + 1))


def along_z(value, hops=1):
    return send(value, lambda y, c, x, z, h: (y, c, x, z + (hops if c == 0 else -hops), h))


def along_x(value):
    return send(value, lambda y, c, x, z, h: (y, c, x + (1 if c == 0 else -1), z, h))


def split3(value):
    parts = []
    for _ in range(3):
        part = lax.reduce_precision(value, 8, 7)
        parts.append(part.astype(jnp.bfloat16))
        value = value - part
    return parts


def split3_in_kernel(value):
    high = value.astype(jnp.bfloat16).astype(jnp.float32)
    middle = (value - high).astype(jnp.bfloat16).astype(jnp.float32)
    return high, middle, value - high - middle


def product_kernel(n_blocks, *refs):
    outward, stay, (head_ref, sent_ref, kept_ref, rows, raw) = refs[:n_blocks], refs[n_blocks:-5], refs[-5:]
    m = sent_ref.shape[0]
    at = 0
    for ref in outward + stay:
        n = ref.shape[0]
        rows[at : at + n] = ref[:, :HALF]
        if at >= m:
            kept_ref[at - m : at - m + n, VOCAB:] = ref[:, HALF:].astype(jnp.float32)
        at += n
    for begin in range(0, VOCAB, TILE):
        columns = slice(begin, begin + TILE)
        part = lax.dot_general(
            rows[...], head_ref[columns, :], (((1,), (1,)), ((), ())), preferred_element_type=jnp.float32
        )
        raw[:, columns] = part[:m]
        kept_ref[:, columns] = part[m:]
    at = 0
    for ref in outward:
        for begin in range(0, ref.shape[0], 32):
            part = slice(at, at + 32)
            value = raw[part, :]
            high = jnp.max(value, axis=1, keepdims=True)
            low = jnp.min(value, axis=1, keepdims=True)
            centre = 0.5 * (high + low)
            unit = jnp.maximum((high - low) * (0.5 / REACH), 1e-30)
            sent_ref[part, :VOCAB] = jnp.exp((value - centre) * (1.0 / unit)).astype(jnp.bfloat16)
            lane = lax.broadcasted_iota(jnp.int32, (32, LANES), 1)
            extra = ref[begin : begin + 32, HALF:].astype(jnp.float32)
            for where, number in ((0, centre), (6, unit)):
                for i, piece in enumerate(split3_in_kernel(number)):
                    extra = jnp.where(lane == where + i, piece, extra)
            sent_ref[part, VOCAB:] = extra.astype(jnp.bfloat16)
            at += 32


def product(outward, stay, head):
    m = sum(a.shape[0] for a in outward)
    return pl.pallas_call(
        functools.partial(product_kernel, len(outward)),
        in_specs=[WHOLE] * (2 * len(outward) + 1),
        out_specs=[WHOLE] * 2,
        out_shape=[
            jax.ShapeDtypeStruct((m, VOCAB + LANES), jnp.bfloat16),
            jax.ShapeDtypeStruct((m, VOCAB + LANES), jnp.float32),
        ],
        scratch_shapes=[pltpu.VMEM((2 * m, HALF), jnp.bfloat16), pltpu.VMEM((m, VOCAB), jnp.float32)],
        compiler_params=pltpu.CompilerParams(vmem_limit_bytes=30 * 2**20),
        cost_estimate=pl.CostEstimate(flops=1, bytes_accessed=1, transcendentals=0),
        name="product",
    )(*outward, *stay, head)


def join_kernel(places, n_got, *refs):
    got, kept, (logits_ref, stats_ref, total) = refs[:n_got], refs[n_got:-3], refs[-3:]
    core, x, z = (lax.axis_index(a) for a in ("core", "x", "z"))
    mine = jnp.where(core == 0, -1, 1)
    for first, refs in ((True, got), (False, kept)):
        for ref, groups in zip(refs, places):
            for begin, blocks in zip(range(0, ref.shape[0], 64), groups):
                value = ref[begin : begin + 64, :VOCAB].astype(jnp.float32)
                extra = ref[begin : begin + 64, VOCAB:].astype(jnp.float32)
                if first:
                    lane = lax.broadcasted_iota(jnp.int32, extra.shape, 1)
                    centre = jnp.sum(jnp.where(lane < 3, extra, 0.0), axis=1, keepdims=True)
                    unit = jnp.sum(jnp.where(lane < 6, 0.0, extra), axis=1, keepdims=True)
                    extra = jnp.where((lane >= 3) & (lane < 6), extra, 0.0)
                    value = jnp.log(value) * unit + centre
                for i, (c, dx, (dz, sz)) in enumerate(blocks):
                    x_at = lax.rem(x + dx + NX, NX)
                    z_at = lax.rem(z + dz + sz * mine + NZ, NZ)
                    at = pl.ds(pl.multiple_of(((c * NX + x_at) * NZ + z_at) * 8, 8), 8)
                    eight = slice(8 * i, 8 * i + 8)
                    if first:
                        total[at, :VOCAB] = value[eight]
                        total[at, VOCAB:] = extra[eight]
                    else:
                        total[at, :VOCAB] += value[eight]
                        total[at, VOCAB:] += extra[eight]
    step = 128
    for begin in range(0, ROWS, step):
        rows = slice(begin, begin + step)
        lane = lax.broadcasted_iota(jnp.int32, (step, LANES), 1)
        squares = jnp.sum(total[rows, VOCAB:], axis=1, keepdims=True)
        inv_rms = lax.rsqrt(squares / D + epsilon)
        logits = total[rows, :VOCAB] * inv_rms
        top = jnp.max(logits, axis=1, keepdims=True)
        summed = jnp.sum(jnp.exp(logits - top), axis=1, keepdims=True)
        logits_ref[rows, :] = logits
        pair = jnp.where(lane == 0, top, summed)
        pair = pair.T
        at = begin // step
        stats_ref[at : at + 1, :] = pair[:1]
        stats_ref[4 + at : 5 + at, :] = pair[1:2]


def join(places, got, kept):
    return pl.pallas_call(
        functools.partial(join_kernel, places, len(got)),
        in_specs=[WHOLE] * (len(got) + len(kept)),
        out_specs=[WHOLE] * 2,
        out_shape=[
            jax.ShapeDtypeStruct((ROWS, VOCAB), jnp.float32),
            jax.ShapeDtypeStruct((8, LANES), jnp.float32),
        ],
        scratch_shapes=[pltpu.VMEM((ROWS, VOCAB + LANES), jnp.float32)],
        compiler_params=pltpu.CompilerParams(vmem_limit_bytes=30 * 2**20),
        name="join",
    )(*got, *kept)


def local(tokens, gain, head):
    yh, core, h = (lax.axis_index(a) for a in ("yh", "core", "h"))
    f32 = tokens.astype(jnp.float32)
    wide = lax.optimization_barrier(jnp.broadcast_to(gain, tokens.shape))
    scaled = (f32 * wide.astype(jnp.float32)).astype(jnp.bfloat16)
    squares = jnp.sum(jnp.square(f32), axis=1)
    pieces = jnp.stack(split3(squares), axis=1)
    own = jnp.concatenate([scaled, jnp.pad(pieces, ((0, 0), (3, LANES - 6)))], axis=1)

    first = core == 0

    def cat(*arrays):
        return jnp.concatenate(arrays)

    def by_core(mine, other):
        return jnp.where(first, mine, other), jnp.where(first, other, mine)

    from_y = send(own, lambda y, c, x, z, h: (y + 1, c, x, z, h))
    from_c = to_core(own)
    from_yc = send(own, lambda y, c, x, z, h: (y + 1, c + 1, x, z, h))
    stays = yh == h
    out_mine, out_other = jnp.where(stays, from_y, own), jnp.where(stays, from_yc, from_c)
    stay_mine, stay_other = jnp.where(stays, own, from_y), jnp.where(stays, from_c, from_yc)
    out16 = cat(*by_core(out_mine, out_other))
    stay16 = cat(*by_core(stay_mine, stay_other))

    after = lax.optimization_barrier

    planes = []
    for own16, own8 in ((out16, out_mine), (stay16, stay_mine)):
        side = cat(along_x(own16), send(own8, lambda y, c, x, z, h: (y, c, x + 2, z, h)))
        other_side = to_core(side)
        parts = by_core(side[:16], other_side[:16]) + by_core(side[16:], other_side[16:])
        planes.append(cat(own16, *parts))

    got, kept = [], []

    def work(outward, stay):
        sent, rest = product(outward, stay, head)
        got.append(to_hid(sent))
        kept.append(rest)
        return sent

    out, stay = (along_z(a) for a in planes)
    sent = work(planes[:1], planes[1:])
    out, sent = after((out, sent))
    for step in range(1, 4):
        out_later = along_z(out if step < 3 else jnp.where(first, out[:32], out[32:]))
        out_other = to_core(out)
        stay, sent = after((stay, sent))
        if step > 1:
            stay, got[step - 2] = after((stay, got[step - 2]))
        stay_later = along_z(stay if step < 3 else jnp.where(first, stay[:32], stay[32:]))
        sent = work([out, out_other], [stay, to_core(stay)])
        out, stay = out_later, stay_later
    out_other = to_core(out)
    stay, sent, got[2] = after((stay, sent, got[2]))
    work([cat(*by_core(out, out_other))], [cat(*by_core(stay, to_core(stay)))])

    def rows_of(*shifts):
        return [[(c, dx, shift) for dx in (0, -1, 1, 2) for c in range(NC)] for shift in shifts]

    places = [rows_of((0, 0))] + [rows_of((0, step), (0, -step)) for step in range(1, 4)] + [rows_of((4, 0))]
    logits, stats = join(places, got, kept)

    def merge(pairs):
        best = jnp.max(pairs[:, :4], axis=0)
        return jnp.concatenate([best, jnp.sum(pairs[:, 4:] * jnp.exp(pairs[:, :4] - best), axis=0)])

    section = [stats] + [
        send(stats, lambda y, c, x, z, h: (y + dy, c + dc, x, z, h)) for dy, dc in ((0, 1), (1, 0), (1, 1))
    ]
    stats = merge(jnp.stack(section))
    every = lax.all_to_all(jnp.broadcast_to(stats[None], (NX * NZ, 8, LANES)), ("x", "z"), 0, 0, tiled=True)
    stats = merge(every)
    top, total = stats[:4].reshape(ROWS, 1), stats[4:].reshape(ROWS, 1)
    return logits - top - jnp.log(total)


def solution(mesh):
    fine = Mesh(mesh.devices.reshape(SIZES), AXES)
    rows = ("yh", "core", "x", "z")
    return jax.shard_map(
        local,
        mesh=fine,
        in_specs=(P(rows, "h"), P("h"), P(rows, "h")),
        out_specs=P("h", rows),
        check_vma=False,
    )
```
